256 devices in a mesh: rep: 2 (over x_hi), fsdp: 128 (over x_lo, y, z, core).
Axes of the slice: x: 4 (x_hi: 2, x_lo: 2; x = x_hi * 2 + x_lo), y: 4, z: 8, core: 2. Of those that a mesh axis runs over, the one named last changes fastest.
Arguments:
- inputs: bfloat16 [163840, 8192], P(('rep', 'fsdp')), may hold values from -6 to 6
- cotangent: bfloat16 [163840, 512], P(('rep', 'fsdp')), may hold values from -0.01953125 to 0.01953125
- weight: float32 [2, 8192, 512], P('rep', 'fsdp'), may hold values from -0.0625 to 0.0625
- first: float32 [2, 8192, 512], P('rep', 'fsdp'), may hold values from -3 to 3
- second: float32 [2, 8192, 512], P('rep', 'fsdp'), may hold values from 0.05 to 2
- roster_step: int32 [2], P('rep'), may hold values from 1 to 64
- anchor: float32 [8192, 512], P('fsdp'), may hold values from -0.0625 to 0.0625
- drift: float32 [2, 8192, 512], P('rep', 'fsdp'), may hold values from -3 to 3
- momentum: float32 [8192, 512], P('fsdp'), may hold values from -3 to 3
Outputs:
- new_weight: float32 [2, 8192, 512], P('rep', 'fsdp')
- new_first: float32 [2, 8192, 512], P('rep', 'fsdp')
- new_second: float32 [2, 8192, 512], P('rep', 'fsdp')
- adam_step: float32 [2, 8192, 512], P('rep', 'fsdp')
- new_anchor: float32 [8192, 512], P('fsdp')
- new_momentum: float32 [8192, 512], P('fsdp')
The draws below stay inside these ranges and needn't reach their ends.
All inputs are finite; a program needn't handle non-finite values.
Results may differ from the reference program's by a relative error of at most 0.00085.
Values may be sent and summed in bfloat16 or wider, within the bound.
No kernel may reach another device: no remote copies, remote signals or barrier semaphores. Data moves between devices by JAX's collectives and lax.ppermute only.
A program may use at most 128 MiB of HBM per device.

```python
import math
import jax
import jax.numpy as jnp
from jax import lax

D = 8192
KV = 512
TOK_REP = 81920
TOKENS = 163840
N_REP = 2


def levels(stream_key, extent, split, low, top_value):
    gain = 1.0
    for position, shards_of in split:
        draws = jax.random.uniform(jax.random.fold_in(jax.random.fold_in(stream_key, 6), position), (shards_of,), jnp.float32, low / len(split), top_value / len(split))
        gain = gain * jnp.repeat(jnp.exp(draws), extent[position] // shards_of).reshape((-1,) + (1,) * (len(extent) - 1 - position))
    return gain


def noise(rng, shape, deviation, reach, split=(), kind=jnp.bfloat16):
    level = levels(rng, shape, split, -0.22, 0.18) if split else 1.0
    array = jax.random.normal(rng, shape, jnp.float32) * deviation * level
    return jnp.minimum(jnp.maximum(array, -reach), reach).astype(kind)


def setup_inputs(seed: int = 0) -> dict:
    splits = jax.random.split(jax.random.key(seed), 10)
    inputs = noise(splits[0], (TOKENS, D), 1.0, 6.0, ((0, 256),))
    cotangent = noise(splits[1], (TOKENS, KV), (TOK_REP ** -0.5), 0.01953125, ((0, 256),))
    weight = noise(splits[2], (N_REP, D, KV), D ** -0.5, 0.0625, ((0, 2), (1, 128)), jnp.float32)
    first = noise(splits[3], (N_REP, D, KV), 0.5, 3.0, ((0, 2), (1, 128)), jnp.float32)
    second = jnp.clip(jnp.exp(math.log(2.0) - 3.6888794 * jax.random.uniform(splits[4], (N_REP, D, KV), jnp.float32) ** levels(splits[4], (N_REP, D, KV), ((0, 2), (1, 128)), -0.2, 0.2)), 0.05, 2.0)
    roster_step = jax.random.randint(splits[5], (N_REP,), 1, 65).astype(jnp.int32)
    anchor = noise(splits[6], (D, KV), D ** -0.5, 0.0625, ((0, 128),), jnp.float32)
    drift = noise(splits[7], (N_REP, D, KV), 0.5, 3.0, ((0, 2), (1, 128)), jnp.float32)
    momentum = noise(splits[8], (D, KV), 0.5, 3.0, ((0, 128),), jnp.float32)
    return dict(inputs=inputs, cotangent=cotangent, weight=weight, first=first, second=second, roster_step=roster_step, anchor=anchor, drift=drift, momentum=momentum)


def inner_update(rows_in, rows_cot, master, first_m, second_m, step_f):
    cast = master.astype(jnp.bfloat16)
    pre = jnp.dot(rows_in, cast, preferred_element_type=jnp.float32)
    sig = jax.nn.sigmoid(pre)
    slope = sig * (1.0 + pre * (1.0 - sig))
    error = (rows_cot.astype(jnp.float32) * slope).astype(jnp.bfloat16)
    grad = lax.dot_general(rows_in, error, (((0,), (0,)), ((), ())), preferred_element_type=jnp.float32)
    new_first = 0.9 * first_m + 0.1 * grad
    new_second = 0.95 * second_m + 0.05 * grad * grad
    corr_one = 1.0 - jnp.power(jnp.float32(0.9), step_f)
    corr_two = 1.0 - jnp.power(jnp.float32(0.95), step_f)
    adam_step = new_first / corr_one / (jnp.sqrt(new_second / corr_two) + 1e-08)
    new_weight = master - 0.0003 * (adam_step + 0.1 * master)
    return (new_weight, new_first, new_second, adam_step)

def reference(inputs, cotangent, weight, first, second, roster_step, anchor, drift, momentum):
    results = []
    for rep_index in range(N_REP):
        lo = rep_index * TOK_REP
        step_f = roster_step[rep_index].astype(jnp.float32)
        results.append(inner_update(inputs[lo:lo + TOK_REP], cotangent[lo:lo + TOK_REP], weight[rep_index], first[rep_index], second[rep_index], step_f))
    new_weight = jnp.stack([item[0] for item in results])
    new_first = jnp.stack([item[1] for item in results])
    new_second = jnp.stack([item[2] for item in results])
    adam_step = jnp.stack([item[3] for item in results])
    delta = -lax.optimization_barrier(jnp.sum(drift, axis=0)) / N_REP
    new_momentum = 0.9 * momentum + delta
    new_anchor = anchor - 0.7 * (delta + 0.9 * new_momentum)
    return (new_weight, new_first, new_second, adam_step, new_anchor, new_momentum)
```

```python
import jax
import jax.numpy as jnp
from jax import lax
from jax.experimental import pallas as pl
from jax.experimental.pallas import tpu as pltpu
from jax.sharding import Mesh, PartitionSpec as P

AXES = ("r", "x", "y", "z", "c")
SIZES = (2, 2, 4, 8, 2)
D = 8192
HALF = 4096
KV = 512
PART = 256
LINE = 1024
TOK = 640
PART_SCALE = 256.0
PLANE_SCALE = 64.0


def swap(value, axis):
    return lax.ppermute(value, axis, [(0, 1), (1, 0)])


def corner(value, flip):
    pairs = []
    for x in range(2):
        for c in range(2):
            pairs.append((2 * x + c, 2 * ((1 - c) if flip else c) + x))
    return lax.ppermute(value, ("x", "c"), pairs)


def corner_back(value, flip):
    pairs = []
    for x in range(2):
        for c in range(2):
            pairs.append((2 * ((1 - c) if flip else c) + x, 2 * x + c))
    return lax.ppermute(value, ("x", "c"), pairs)


def shift(value, axis, size, step):
    return lax.ppermute(value, axis, [(i, (i + step) % size) for i in range(size)])


def pre_kernel(place_ref, *refs):
    columns, weights, o_ref = refs[:4], refs[4:8], refs[8]
    total = jnp.dot(columns[0][...], weights[0][...], preferred_element_type=jnp.float32)
    for column, part in zip(columns[1:], weights[1:]):
        total = total + jnp.dot(column[...], part[...], preferred_element_type=jnp.float32)
    o_ref[...] = total


def project(place, columns, weights):
    rows = 320

    def column_spec(step):
        return pl.BlockSpec((rows, LINE), lambda i, p: (i, p[0] + lax.rem(p[1] + step, 4)))

    return pl.pallas_call(
        pre_kernel,
        grid_spec=pltpu.PrefetchScalarGridSpec(
            num_scalar_prefetch=1,
            grid=(TOK // rows,),
            in_specs=[column_spec(step) for step in range(4)] + [pl.BlockSpec((LINE, PART), lambda i, p: (0, 0))] * 4,
            out_specs=pl.BlockSpec((rows, PART), lambda i, p: (i, 0)),
        ),
        out_shape=jax.ShapeDtypeStruct((TOK, PART), jnp.float32),
        compiler_params=pltpu.CompilerParams(vmem_limit_bytes=16 * 1024 * 1024),
        cost_estimate=pl.CostEstimate(
            flops=2 * TOK * HALF * PART, bytes_accessed=2 * TOK * HALF + 2 * HALF * PART + 4 * TOK * PART, transcendentals=0
        ),
    )(place, *[columns] * 4, *weights)


def error_kernel(own_ref, got_ref, cot_ref, o_ref):
    pre = own_ref[...] + got_ref[...]
    sig = jax.nn.sigmoid(pre)
    slope = sig * (1.0 + pre * (1.0 - sig))
    error = cot_ref[...].astype(jnp.float32) * slope
    o_ref[...] = error.T.astype(jnp.bfloat16)


def error_of(own, got, cotangent, part):
    return pl.pallas_call(
        error_kernel,
        grid=(1,),
        in_specs=[
            pl.BlockSpec((TOK, PART), lambda i: (0, 0)),
            pl.BlockSpec((TOK, PART), lambda i: (0, 0)),
            pl.BlockSpec((TOK, PART), lambda i: (0, part)),
        ],
        out_specs=pl.BlockSpec((PART, TOK), lambda i: (0, 0)),
        out_shape=jax.ShapeDtypeStruct((PART, TOK), jnp.bfloat16),
        compiler_params=pltpu.CompilerParams(vmem_limit_bytes=16 * 1024 * 1024),
        cost_estimate=pl.CostEstimate(flops=8 * TOK * PART, bytes_accessed=12 * TOK * PART, transcendentals=TOK * PART),
    )(own, got, cotangent)


def grad_kernel(own_ref, other_ref, xo_ref, xr_ref, eo_ref, er_ref, o_ref):
    part = jnp.dot(eo_ref[...], xo_ref[...], preferred_element_type=jnp.float32)
    part = part + jnp.dot(er_ref[...], xr_ref[...], preferred_element_type=jnp.float32)
    for k in range(o_ref.shape[0]):
        o_ref[k] = part[:, 128 * k : 128 * (k + 1)]


def gradient(own_place, other_place, own, other, err_own, err_other, step):
    width = 512
    count = LINE // width

    def column_spec(which):
        def index(i, a, b):
            p = (a, b)[which]
            return (0, (p[0] + lax.rem(p[1] + step, 4)) * count + i)

        return pl.BlockSpec((TOK, width), index)

    e_spec = pl.BlockSpec((PART, TOK), lambda i, a, b: (0, 0))
    return pl.pallas_call(
        grad_kernel,
        grid_spec=pltpu.PrefetchScalarGridSpec(
            num_scalar_prefetch=2,
            grid=(count,),
            in_specs=[column_spec(0), column_spec(1), e_spec, e_spec],
            out_specs=pl.BlockSpec((width // 128, PART, 128), lambda i, a, b: (i, 0, 0)),
        ),
        out_shape=jax.ShapeDtypeStruct((LINE // 128, PART, 128), jnp.float32),
        compiler_params=pltpu.CompilerParams(vmem_limit_bytes=16 * 1024 * 1024),
        cost_estimate=pl.CostEstimate(
            flops=4 * TOK * LINE * PART, bytes_accessed=4 * TOK * LINE + 4 * LINE * PART, transcendentals=0
        ),
    )(own_place, other_place, own, other, err_own, err_other)


def turn_kernel(x_ref, i_ref, a_ref, b_ref):
    total = i_ref[...].T * (1.0 / PLANE_SCALE)
    low, high = total[:64], total[64:]
    flag = jnp.full(low.shape, x_ref[0], jnp.int32) == 0
    a_ref[...] = jnp.where(flag, low, high)
    b_ref[...] = jnp.where(flag, high, low)


def turn(place, value):
    vmem = pl.BlockSpec(memory_space=pltpu.VMEM)
    return pl.pallas_call(
        turn_kernel,
        in_specs=[pl.BlockSpec(memory_space=pltpu.SMEM), vmem],
        out_specs=[vmem] * 2,
        out_shape=[jax.ShapeDtypeStruct((64, PART), jnp.float32)] * 2,
    )(place, value)


def adam_kernel(s_ref, a0_ref, b0_ref, a1_ref, b1_ref, w_ref, m_ref, v_ref, nw_ref, nm_ref, nv_ref, st_ref):
    grad = jnp.concatenate([a0_ref[...] + b0_ref[...], a1_ref[...] + b1_ref[...]], axis=1)
    master = w_ref[...]
    new_first = 0.9 * m_ref[...] + 0.1 * grad
    new_second = 0.95 * v_ref[...] + 0.05 * grad * grad
    step = new_first / s_ref[0] / (jnp.sqrt(new_second / s_ref[1]) + 1e-08)
    nw_ref[...] = master - 0.0003 * (step + 0.1 * master)
    nm_ref[...] = new_first
    nv_ref[...] = new_second
    st_ref[...] = step


def adam(corr, pieces, master, first, second):
    shape = jax.ShapeDtypeStruct(master.shape, jnp.float32)
    vmem = pl.BlockSpec(memory_space=pltpu.VMEM)
    return pl.pallas_call(
        adam_kernel,
        in_specs=[pl.BlockSpec(memory_space=pltpu.SMEM)] + [vmem] * 7,
        out_specs=[vmem] * 4,
        out_shape=[shape] * 4,
    )(corr, *pieces, master, first, second)


def gather_line(block):
    column = lax.all_to_all(jnp.broadcast_to(block[None], (8, 128, PART)), "z", 0, 0, tiled=True)
    return column.reshape(1024, PART)


def gather_plane(column):
    return [column] + [shift(column, "y", 4, -step) for step in (1, 2, 3)]


def scatter_plane(pieces):
    got = []
    for step in (2, 1, 3):
        got.append(shift((pieces[step] * PART_SCALE).astype(jnp.float16), "y", 4, step))
    return pieces[0] * PLANE_SCALE + sum(g.astype(jnp.float32) for g in got) * (PLANE_SCALE / PART_SCALE)


def scatter_line(line):
    return lax.all_to_all(line.astype(jnp.float16), "z", 0, 0, tiled=True)


def finish(place, got):
    a, b = turn(place, jnp.sum(got.astype(jnp.float32), axis=0))
    return corner_back(a, False), corner_back(b, True)


def on_device(inputs, cotangent, weight, first, second, roster_step, anchor, drift, momentum):
    q = lax.axis_index("c").astype(jnp.int32)
    y = lax.axis_index("y").astype(jnp.int32)
    x = lax.axis_index("x").astype(jnp.int32)
    own_place = jnp.stack([q * 4, y])
    other_place = jnp.stack([y * 0, y])
    x_place = x.reshape(1)
    at_zero = x == 0
    master = weight[0]
    cast = master.astype(jnp.bfloat16)
    a = corner(cast, False)
    b = corner(cast, True)
    send = lax.dynamic_slice(inputs, (0, (1 - q) * HALF), (TOK, HALF))
    block = jnp.concatenate([jnp.where(at_zero, a, b), jnp.where(at_zero, b, a)], axis=0)
    block, send = lax.optimization_barrier((block, send))
    other = swap(send, "c")
    drift_other = swap(drift[0], "r")

    line0 = gather_line(block[:, :PART])
    line0, block, drift_other = lax.optimization_barrier((line0, block, drift_other))
    line1 = gather_line(block[:, PART:])

    def compute(line, part):
        half = gather_plane(line)
        pre_other = project(other_place, other, half)
        got = swap(pre_other, "c")
        pre = project(own_place, inputs, half)
        error = error_of(pre, got, cotangent, part)
        error_other = swap(error, "c")
        return [gradient(own_place, other_place, inputs, other, error, error_other, step) for step in range(4)]

    g0 = scatter_plane(compute(line0, 0))
    g1 = scatter_plane(compute(line1, 1))
    t0 = finish(x_place, scatter_line(g0))
    t1 = finish(x_place, scatter_line(g1))

    step_f = roster_step[0].astype(jnp.float32)
    corr = jnp.stack([1.0 - jnp.power(jnp.float32(0.9), step_f), 1.0 - jnp.power(jnp.float32(0.95), step_f)])
    new_weight, new_first, new_second, adam_step = adam(corr, t0 + t1, master, first[0], second[0])

    delta = -(drift[0] + drift_other) / 2
    new_momentum = 0.9 * momentum + delta
    new_anchor = anchor - 0.7 * (delta + 0.9 * new_momentum)
    return (new_weight[None], new_first[None], new_second[None], adam_step[None], new_anchor, new_momentum)


def solution(mesh):
    fine = Mesh(mesh.devices.reshape(SIZES), AXES)
    every = ("r", "x", "y", "z", "c")
    fsdp = ("x", "y", "z", "c")
    return jax.shard_map(
        on_device,
        mesh=fine,
        in_specs=(
            P(every, None),
            P(every, None),
            P("r", fsdp, None),
            P("r", fsdp, None),
            P("r", fsdp, None),
            P("r"),
            P(fsdp, None),
            P("r", fsdp, None),
            P(fsdp, None),
        ),
        out_specs=(
            P("r", fsdp, None),
            P("r", fsdp, None),
            P("r", fsdp, None),
            P("r", fsdp, None),
            P(fsdp, None),
            P(fsdp, None),
        ),
        check_vma=False,
    )
```

```python
import jax
import jax.numpy as jnp
from jax import lax
from jax.experimental import pallas as pl
from jax.experimental.pallas import tpu as pltpu
from jax.sharding import Mesh, PartitionSpec as P

AXES = ("r", "x", "y", "z", "c")
SIZES = (2, 2, 4, 8, 2)
D = 8192
HALF = 4096
KV = 512
PART = 256
LINE = 1024
TOK = 640
PART_SCALE = 256.0
PAIR_SCALE = 128.0
PLANE_SCALE = 64.0
WHOLE_SCALE = 32.0
WIDE = 55 * 1024 * 1024
LIGHT = pl.CostEstimate(flops=1000, bytes_accessed=1000, transcendentals=0)


def swap(value, axis):
    return lax.ppermute(value, axis, [(0, 1), (1, 0)])


SIDE = [(1, 0), (2, 3), (0, 2), (3, 1)]
CROSS = [(1, 2), (2, 1)]


def spread(value):
    return lax.ppermute(value, ("x", "c"), SIDE), lax.ppermute(value, ("x", "c"), CROSS)


def collect(side, cross):
    return (
        lax.ppermute(side, ("x", "c"), [(d, s) for s, d in SIDE]),
        lax.ppermute(cross, ("x", "c"), [(d, s) for s, d in CROSS]),
    )


def shift(value, axis, size, step):
    return lax.ppermute(value, axis, [(i, (i + step) % size) for i in range(size)])


def round_kernel(a_ref, b_ref, c_ref, d_ref, line_ref, other_ref, rows_ref, next_ref):
    for i, ref in enumerate((a_ref, b_ref, c_ref, d_ref)):
        rows_ref[i] = ref[...]


def next_round(pieces, line, other):
    vmem = pl.BlockSpec(memory_space=pltpu.VMEM)
    anywhere = pl.BlockSpec(memory_space=pl.ANY)
    return pl.pallas_call(
        round_kernel,
        in_specs=[vmem] * 4 + [anywhere] * 2,
        out_specs=[vmem, anywhere],
        out_shape=[
            jax.ShapeDtypeStruct((4,) + pieces[0].shape, pieces[0].dtype),
            jax.ShapeDtypeStruct(line.shape, line.dtype),
        ],
        input_output_aliases={4: 1},
        cost_estimate=LIGHT,
    )(*pieces, line, other)


def gate_kernel(value_ref, after_ref, o_ref):
    o_ref[0] = value_ref[0]


def gate(value, after):
    smem = pl.BlockSpec(memory_space=pltpu.SMEM)
    return pl.pallas_call(
        gate_kernel,
        in_specs=[smem, pl.BlockSpec(memory_space=pl.ANY)],
        out_specs=smem,
        out_shape=jax.ShapeDtypeStruct((1,), jnp.float32),
        cost_estimate=LIGHT,
    )(jnp.full((1,), value, jnp.float32), after)[0]


def put_in_order(place_ref, own_ref, side_ref, cross_ref, put):
    x, q = place_ref[0], place_ref[1]

    @pl.when(jnp.logical_and(x == 0, q == 0))
    def _():
        put(own_ref, side_ref)

    @pl.when(jnp.logical_and(x == 1, q == 1))
    def _():
        put(side_ref, own_ref)

    @pl.when(jnp.logical_and(x == 1, q == 0))
    def _():
        put(side_ref, cross_ref)

    @pl.when(jnp.logical_and(x == 0, q == 1))
    def _():
        put(cross_ref, side_ref)


def weave_kernel(place_ref, own_ref, side_ref, cross_ref, o_ref):
    def put(low, high):
        o_ref[:, :, :64] = low[...]
        o_ref[:, :, 64:] = high[...]

    put_in_order(place_ref, own_ref, side_ref, cross_ref, put)


def weave(place, own, side, cross):
    vmem = pl.BlockSpec(memory_space=pltpu.VMEM)
    return pl.pallas_call(
        weave_kernel,
        in_specs=[pl.BlockSpec(memory_space=pltpu.SMEM)] + [vmem] * 3,
        out_specs=vmem,
        out_shape=jax.ShapeDtypeStruct((4, 8, 128, PART), jnp.bfloat16),
        compiler_params=pltpu.CompilerParams(vmem_limit_bytes=16 * 1024 * 1024),
        cost_estimate=LIGHT,
    )(place, own, side, cross)


def join_kernel(place_ref, own_ref, side_ref, cross_ref, start_ref, drift_ref, o_ref):
    def put(low, high):
        o_ref[:64] = low[...]
        o_ref[64:] = high[...]

    put_in_order(place_ref, own_ref, side_ref, cross_ref, put)


def join(place, own, side, cross, *after):
    vmem = pl.BlockSpec(memory_space=pltpu.VMEM)
    return pl.pallas_call(
        join_kernel,
        in_specs=[pl.BlockSpec(memory_space=pltpu.SMEM)] + [vmem] * 3 + [pl.BlockSpec(memory_space=pl.ANY)] * 2,
        out_specs=vmem,
        out_shape=jax.ShapeDtypeStruct((128, PART), jnp.bfloat16),
        cost_estimate=LIGHT,
    )(place, own, side, cross, *after)


def pre_kernel(place_ref, *refs):
    columns, first, second, o_ref = refs[:4], refs[4:8], refs[8:12], refs[13]
    for k, weights in enumerate((first, second)):
        total = None
        for column, part in zip(columns, weights):
            term = jnp.dot(column[...], part[...].reshape(LINE, PART), preferred_element_type=jnp.float32)
            total = term if total is None else total + term
        o_ref[:, k * PART : (k + 1) * PART] = total


def project(place, columns, first, second, after):
    rows = 320

    def column_spec(step):
        return pl.BlockSpec((rows, LINE), lambda i, p: (i, p[0] + lax.rem(p[1] + step, 4)))

    weight_specs = [pl.BlockSpec((LINE, PART), lambda i, p: (0, 0))] * 4
    weight_specs += [pl.BlockSpec((1, 8, 128, PART), lambda i, p, s=step: (s, 0, 0, 0)) for step in range(4)]
    return pl.pallas_call(
        pre_kernel,
        grid_spec=pltpu.PrefetchScalarGridSpec(
            num_scalar_prefetch=1,
            grid=(TOK // rows,),
            in_specs=[column_spec(step) for step in range(4)] + weight_specs + [pl.BlockSpec(memory_space=pl.ANY)],
            out_specs=pl.BlockSpec((rows, KV), lambda i, p: (i, 0)),
        ),
        out_shape=jax.ShapeDtypeStruct((TOK, KV), jnp.float32),
        compiler_params=pltpu.CompilerParams(vmem_limit_bytes=WIDE),
        cost_estimate=LIGHT,
    )(place, *[columns] * 4, *first, *[second] * 4, after)


def error_kernel(own_ref, got_ref, cot_ref, o_ref):
    pre = own_ref[...] + got_ref[...]
    sig = jax.nn.sigmoid(pre)
    slope = sig * (1.0 + pre * (1.0 - sig))
    o_ref[...] = (cot_ref[...].astype(jnp.float32) * slope).astype(jnp.bfloat16)


def error_of(own, got, cotangent):
    rows = 160
    block = pl.BlockSpec((rows, KV), lambda i: (i, 0))
    return pl.pallas_call(
        error_kernel,
        grid=(TOK // rows,),
        in_specs=[block] * 3,
        out_specs=block,
        out_shape=jax.ShapeDtypeStruct((TOK, KV), jnp.bfloat16),
        compiler_params=pltpu.CompilerParams(vmem_limit_bytes=16 * 1024 * 1024),
        cost_estimate=LIGHT,
    )(own, got, cotangent)


def grad_kernel(place_ref, xo_ref, xr_ref, eo_ref, er_ref, first_ref, second_ref):
    dims = (((0,), (0,)), ((), ()))
    part = lax.dot_general(xo_ref[...], eo_ref[...], dims, preferred_element_type=jnp.float32)
    part = part + lax.dot_general(xr_ref[...], er_ref[...], dims, preferred_element_type=jnp.float32)
    first_ref[...] = part[:, :PART]
    second_ref[...] = part[:, PART:]


def gradient(place, own, other, err_own, err_other):
    width = 1024
    each = LINE // width
    x_spec = pl.BlockSpec((TOK, width), lambda i, p: (0, p[0] * each + i))
    e_spec = pl.BlockSpec((TOK, KV), lambda i, p: (0, 0))
    shape = jax.ShapeDtypeStruct((HALF, PART), jnp.float32)
    first, second = pl.pallas_call(
        grad_kernel,
        grid_spec=pltpu.PrefetchScalarGridSpec(
            num_scalar_prefetch=1,
            grid=(4 * each,),
            in_specs=[x_spec, x_spec, e_spec, e_spec],
            out_specs=[
                pl.BlockSpec((width, PART), lambda i, p: (i, 0)),
                pl.BlockSpec((width, PART), lambda i, p: (lax.rem(i // each + 4 - p[1], 4) * each + lax.rem(i, each), 0)),
            ],
        ),
        out_shape=[shape, shape],
        compiler_params=pltpu.CompilerParams(vmem_limit_bytes=WIDE),
        cost_estimate=LIGHT,
    )(place, own, other, err_own, err_other)
    return first.reshape(4, 8, 128, PART), second.reshape(4, 8, 128, PART)


def adam_kernel(s_ref, g0_ref, g1_ref, w_ref, m_ref, v_ref, nw_ref, nm_ref, nv_ref, st_ref):
    grad = jnp.concatenate([g0_ref[...], g1_ref[...]], axis=1)
    master = w_ref[...]
    new_first = 0.9 * m_ref[...] + 0.1 * grad
    new_second = 0.95 * v_ref[...] + 0.05 * grad * grad
    step = new_first / s_ref[0] / (jnp.sqrt(new_second / s_ref[1]) + 1e-08)
    nw_ref[...] = master - 0.0003 * (step + 0.1 * master)
    nm_ref[...] = new_first
    nv_ref[...] = new_second
    st_ref[...] = step


def adam(corr, pieces, master, first, second):
    shape = jax.ShapeDtypeStruct(master.shape, jnp.float32)
    vmem = pl.BlockSpec(memory_space=pltpu.VMEM)
    return pl.pallas_call(
        adam_kernel,
        in_specs=[pl.BlockSpec(memory_space=pltpu.SMEM)] + [vmem] * 5,
        out_specs=[vmem] * 4,
        out_shape=[shape] * 4,
    )(corr, *pieces, master, first, second)


def gather_line(block):
    rows = block.shape[0]
    column = lax.all_to_all(jnp.broadcast_to(block[None], (8, rows, PART)), "z", 0, 0, tiled=True)
    return column.reshape(8 * rows, PART)


def gather_plane(column):
    got = {step: shift(column, "y", 4, -step) for step in (2, 1, 3)}
    return [column, got[1], got[2], got[3]]


def send_plane(pieces, scale):
    return [shift((pieces[step - 1] * scale).astype(jnp.float16), "y", 4, step) for step in (2, 1, 3)]


def total_of(own, got, scale):
    return own + sum(g.astype(jnp.float32) for g in got) * (1.0 / scale)


def scatter_line(total, scale, applied=None):
    total = total * (scale if applied is None else applied)
    got = lax.all_to_all(total.astype(jnp.float16), "z", 0, 0, tiled=True)
    return jnp.sum(got.astype(jnp.float32), axis=0) * (1.0 / scale)


def on_device(inputs, cotangent, weight, first, second, roster_step, anchor, drift, momentum):
    q = lax.axis_index("c").astype(jnp.int32).reshape(1)
    y = lax.axis_index("y").astype(jnp.int32).reshape(1)
    x = lax.axis_index("x").astype(jnp.int32).reshape(1)
    place = jnp.concatenate([x, q])
    level = (x == q)[0]
    first_core = (q == 0)[0]
    master = weight[0]
    cast = master.astype(jnp.bfloat16)
    start = gather_line(cast[:, PART:])
    side, cross = spread(cast[:, :PART])
    drift_other = swap(drift[0], "r")
    other = swap(inputs, "c")
    block = join(place, cast[:, :PART], side, cross, start, drift_other)
    column = gather_plane(start)
    rows, line = next_round(column, gather_line(block), other)
    half0 = gather_plane(line)
    rows = rows.reshape(4, 8, 64, PART)
    half1 = weave(place, rows, *spread(rows))

    delta = -(drift[0] + drift_other) / 2
    new_momentum = 0.9 * momentum + delta
    new_anchor = anchor - 0.7 * (delta + 0.9 * new_momentum)

    at = jnp.concatenate([4 * q, y])
    pre_other = project(at, other, half0, half1, q)
    got = swap(pre_other, "c")
    pre = project(at, inputs, half0, half1, pre_other)
    error = error_of(pre, got, cotangent)
    error_other = swap(error, "c")
    whole0, whole1 = gradient(at, inputs, other, error, error_other)
    got0 = lax.all_to_all((whole0 * PART_SCALE).astype(jnp.float16), "y", 0, 0, tiled=True)
    low, high = whole1[:, :, :64], whole1[:, :, 64:]
    same, else_ = jnp.where(first_core, low, high), jnp.where(first_core, high, low)
    side_out = (jnp.where(level, else_, same) * PART_SCALE).astype(jnp.float16)
    cross_out = (else_ * PART_SCALE).astype(jnp.float16)
    side, cross = collect(side_out, cross_out)
    met1 = jnp.where(level, same, cross.astype(jnp.float32) * (1.0 / PART_SCALE)) + side.astype(jnp.float32) * (
        1.0 / PART_SCALE
    )
    sent1 = send_plane(met1[1:], PAIR_SCALE)

    total0 = jnp.sum(got0.astype(jnp.float32), axis=0) * (1.0 / PART_SCALE)
    total0 = scatter_line(total0, PLANE_SCALE)
    low, high = total0[:64], total0[64:]
    same, else_ = jnp.where(first_core, low, high), jnp.where(first_core, high, low)
    side, cross = collect(jnp.where(level, else_, same), else_)
    first0 = side + jnp.where(level, same, cross)
    total1 = scatter_line(total_of(met1[0], sent1, PAIR_SCALE), WHOLE_SCALE, gate(WHOLE_SCALE, total0))

    step_f = roster_step[0].astype(jnp.float32)
    corr = jnp.stack([1.0 - jnp.power(jnp.float32(0.9), step_f), 1.0 - jnp.power(jnp.float32(0.95), step_f)])
    new_weight, new_first, new_second, adam_step = adam(corr, (first0, total1), master, first[0], second[0])
    return (new_weight[None], new_first[None], new_second[None], adam_step[None], new_anchor, new_momentum)


def solution(mesh):
    fine = Mesh(mesh.devices.reshape(SIZES), AXES)
    every = ("r", "x", "y", "z", "c")
    fsdp = ("x", "y", "z", "c")
    return jax.shard_map(
        on_device,
        mesh=fine,
        in_specs=(
            P(every, None),
            P(every, None),
            P("r", fsdp, None),
            P("r", fsdp, None),
            P("r", fsdp, None),
            P("r"),
            P(fsdp, None),
            P("r", fsdp, None),
            P(fsdp, None),
        ),
        out_specs=(
            P("r", fsdp, None),
            P("r", fsdp, None),
            P("r", fsdp, None),
            P("r", fsdp, None),
            P(fsdp, None),
            P(fsdp, None),
        ),
        check_vma=False,
    )
```

```python
import functools

import jax
import jax.numpy as jnp
from jax import lax
from jax.experimental import pallas as pl
from jax.experimental.pallas import tpu as pltpu
from jax.sharding import Mesh, PartitionSpec as P

AXES = ("r", "x", "y", "z", "c")
SIZES = (2, 2, 4, 8, 2)
D = 8192
HALF = 4096
KV = 512
PART = 256
LINE = 1024
TOK = 640
PART_SCALE = 256.0
PAIR_SCALE = 128.0
PLANE_SCALE = 64.0
WHOLE_SCALE = 32.0
WIDE = 20 * 1024 * 1024
LIGHT = pl.CostEstimate(flops=1000, bytes_accessed=1000, transcendentals=0)


def swap(value, axis):
    return lax.ppermute(value, axis, [(0, 1), (1, 0)])


SIDE = [(1, 0), (2, 3), (0, 2), (3, 1)]
CROSS = [(1, 2), (2, 1)]


def spread(value):
    return lax.ppermute(value, ("x", "c"), SIDE), lax.ppermute(value, ("x", "c"), CROSS)


def collect(side, cross):
    return (
        lax.ppermute(side, ("x", "c"), [(d, s) for s, d in SIDE]),
        lax.ppermute(cross, ("x", "c"), [(d, s) for s, d in CROSS]),
    )


def shift(value, axis, size, step):
    return lax.ppermute(value, axis, [(i, (i + step) % size) for i in range(size)])


def round_kernel(a_ref, b_ref, c_ref, line_ref, side_ref, cross_ref, rows_ref, next_ref):
    for i, ref in enumerate((a_ref, b_ref, c_ref)):
        rows_ref[i] = ref[...]


def next_round(pieces, line, side, cross):
    vmem = pl.BlockSpec(memory_space=pltpu.VMEM)
    anywhere = pl.BlockSpec(memory_space=pl.ANY)
    return pl.pallas_call(
        round_kernel,
        in_specs=[vmem] * 3 + [anywhere] * 3,
        out_specs=[vmem, anywhere],
        out_shape=[
            jax.ShapeDtypeStruct((3,) + pieces[0].shape, pieces[0].dtype),
            jax.ShapeDtypeStruct(line.shape, line.dtype),
        ],
        input_output_aliases={3: 1},
        cost_estimate=LIGHT,
    )(*pieces, line, side, cross)


def gate_kernel(value_ref, after_ref, o_ref):
    o_ref[0] = value_ref[0]


def gate(value, after):
    smem = pl.BlockSpec(memory_space=pltpu.SMEM)
    return pl.pallas_call(
        gate_kernel,
        in_specs=[smem, pl.BlockSpec(memory_space=pl.ANY)],
        out_specs=smem,
        out_shape=jax.ShapeDtypeStruct((1,), jnp.float32),
        cost_estimate=LIGHT,
    )(jnp.full((1,), value, jnp.float32), after)[0]


def put_in_order(place_ref, own_ref, side_ref, cross_ref, put):
    x, q = place_ref[0], place_ref[1]

    @pl.when(jnp.logical_and(x == 0, q == 0))
    def _():
        put(own_ref, side_ref)

    @pl.when(jnp.logical_and(x == 1, q == 1))
    def _():
        put(side_ref, own_ref)

    @pl.when(jnp.logical_and(x == 1, q == 0))
    def _():
        put(side_ref, cross_ref)

    @pl.when(jnp.logical_and(x == 0, q == 1))
    def _():
        put(cross_ref, side_ref)


def weave_kernel(place_ref, own0_ref, side0_ref, cross0_ref, own_ref, side_ref, cross_ref, o_ref):
    def put_near(low, high):
        o_ref[0, :, :64] = low[...]
        o_ref[0, :, 64:] = high[...]

    def put(low, high):
        o_ref[1:, :, :64] = low[...]
        o_ref[1:, :, 64:] = high[...]

    put_in_order(place_ref, own0_ref, side0_ref, cross0_ref, put_near)
    put_in_order(place_ref, own_ref, side_ref, cross_ref, put)


def weave(place, near, rest):
    vmem = pl.BlockSpec(memory_space=pltpu.VMEM)
    return pl.pallas_call(
        weave_kernel,
        in_specs=[pl.BlockSpec(memory_space=pltpu.SMEM)] + [vmem] * 6,
        out_specs=vmem,
        out_shape=jax.ShapeDtypeStruct((4, 8, 128, PART), jnp.bfloat16),
        compiler_params=pltpu.CompilerParams(vmem_limit_bytes=16 * 1024 * 1024),
        cost_estimate=LIGHT,
    )(place, *near, *rest)


def join_kernel(place_ref, own_ref, side_ref, cross_ref, start_ref, drift_ref, other_ref, o_ref):
    def put(low, high):
        o_ref[:64] = low[...]
        o_ref[64:] = high[...]

    put_in_order(place_ref, own_ref, side_ref, cross_ref, put)


def join(place, own, side, cross, *after):
    vmem = pl.BlockSpec(memory_space=pltpu.VMEM)
    return pl.pallas_call(
        join_kernel,
        in_specs=[pl.BlockSpec(memory_space=pltpu.SMEM)] + [vmem] * 3 + [pl.BlockSpec(memory_space=pl.ANY)] * 3,
        out_specs=vmem,
        out_shape=jax.ShapeDtypeStruct((128, PART), jnp.bfloat16),
        cost_estimate=LIGHT,
    )(place, own, side, cross, *after)


def pre_kernel(count, place_ref, *refs):
    columns, weights, o_ref = refs[:count], refs[count : 2 * count], refs[-1]
    total = None if len(refs) == 2 * count + 2 else refs[2 * count][...]
    for column, part in zip(columns, weights):
        term = jnp.dot(column[...], part[...].reshape(LINE, PART), preferred_element_type=jnp.float32)
        total = term if total is None else total + term
    o_ref[...] = total


def project(place, columns, weights, steps, begun, after):
    rows = 320

    def column_spec(step):
        return pl.BlockSpec((rows, LINE), lambda i, p: (i, p[0] + lax.rem(p[1] + step, 4)))

    out = pl.BlockSpec((rows, PART), lambda i, p: (i, 0))
    if isinstance(weights, list):
        weight_specs = [pl.BlockSpec((LINE, PART), lambda i, p: (0, 0))] * len(steps)
    else:
        weight_specs = [pl.BlockSpec((1, 8, 128, PART), lambda i, p, s=step: (s, 0, 0, 0)) for step in steps]
        weights = [weights] * len(steps)
    more = [] if begun is None else [begun]
    return pl.pallas_call(
        functools.partial(pre_kernel, len(steps)),
        grid_spec=pltpu.PrefetchScalarGridSpec(
            num_scalar_prefetch=1,
            grid=(TOK // rows,),
            in_specs=[column_spec(step) for step in steps]
            + weight_specs
            + [out] * len(more)
            + [pl.BlockSpec(memory_space=pl.ANY)],
            out_specs=out,
        ),
        out_shape=jax.ShapeDtypeStruct((TOK, PART), jnp.float32),
        compiler_params=pltpu.CompilerParams(vmem_limit_bytes=WIDE),
        cost_estimate=LIGHT,
    )(place, *[columns] * len(steps), *weights, *more, after)


def error_kernel(own_ref, got_ref, cot_ref, o_ref):
    pre = own_ref[...] + got_ref[...]
    sig = jax.nn.sigmoid(pre)
    slope = sig * (1.0 + pre * (1.0 - sig))
    o_ref[...] = (cot_ref[...].astype(jnp.float32) * slope).astype(jnp.bfloat16)


def error_of(own, got, cotangent, part):
    whole = pl.BlockSpec((TOK, PART), lambda i: (0, 0))
    return pl.pallas_call(
        error_kernel,
        grid=(1,),
        in_specs=[whole, whole, pl.BlockSpec((TOK, PART), lambda i: (0, part))],
        out_specs=whole,
        out_shape=jax.ShapeDtypeStruct((TOK, PART), jnp.bfloat16),
        compiler_params=pltpu.CompilerParams(vmem_limit_bytes=16 * 1024 * 1024),
        cost_estimate=LIGHT,
    )(own, got, cotangent)


def grad_kernel(place_ref, xo_ref, xr_ref, eo0_ref, er0_ref, eo1_ref, er1_ref, first_ref, second_ref):
    dims = (((0,), (0,)), ((), ()))
    own, other = xo_ref[...], xr_ref[...]
    for eo_ref, er_ref, o_ref in ((eo0_ref, er0_ref, first_ref), (eo1_ref, er1_ref, second_ref)):
        part = lax.dot_general(own, eo_ref[...], dims, preferred_element_type=jnp.float32)
        o_ref[...] = part + lax.dot_general(other, er_ref[...], dims, preferred_element_type=jnp.float32)


def gradient(place, own, other, errors):
    width = 1024
    each = LINE // width
    x_spec = pl.BlockSpec((TOK, width), lambda i, p: (0, p[0] * each + i))
    e_spec = pl.BlockSpec((TOK, PART), lambda i, p: (0, 0))
    shape = jax.ShapeDtypeStruct((HALF, PART), jnp.float32)
    first, second = pl.pallas_call(
        grad_kernel,
        grid_spec=pltpu.PrefetchScalarGridSpec(
            num_scalar_prefetch=1,
            grid=(4 * each,),
            in_specs=[x_spec, x_spec] + [e_spec] * 4,
            out_specs=[
                pl.BlockSpec((width, PART), lambda i, p: (i, 0)),
                pl.BlockSpec((width, PART), lambda i, p: (lax.rem(i // each + 4 - p[1], 4) * each + lax.rem(i, each), 0)),
            ],
        ),
        out_shape=[shape, shape],
        compiler_params=pltpu.CompilerParams(vmem_limit_bytes=WIDE),
        cost_estimate=LIGHT,
    )(place, own, other, *errors)
    return first.reshape(4, 8, 128, PART), second.reshape(4, 8, 128, PART)


def adam_kernel(s_ref, g0_ref, g1_ref, w_ref, m_ref, v_ref, nw_ref, nm_ref, nv_ref, st_ref):
    grad = jnp.concatenate([g0_ref[...], g1_ref[...]], axis=1)
    master = w_ref[...]
    new_first = 0.9 * m_ref[...] + 0.1 * grad
    new_second = 0.95 * v_ref[...] + 0.05 * grad * grad
    step = new_first / s_ref[0] / (jnp.sqrt(new_second / s_ref[1]) + 1e-08)
    nw_ref[...] = master - 0.0003 * (step + 0.1 * master)
    nm_ref[...] = new_first
    nv_ref[...] = new_second
    st_ref[...] = step


def adam(corr, pieces, master, first, second):
    shape = jax.ShapeDtypeStruct(master.shape, jnp.float32)
    vmem = pl.BlockSpec(memory_space=pltpu.VMEM)
    return pl.pallas_call(
        adam_kernel,
        in_specs=[pl.BlockSpec(memory_space=pltpu.SMEM)] + [vmem] * 5,
        out_specs=[vmem] * 4,
        out_shape=[shape] * 4,
    )(corr, *pieces, master, first, second)


def gather_line(block):
    rows = block.shape[0]
    column = lax.all_to_all(jnp.broadcast_to(block[None], (8, rows, PART)), "z", 0, 0, tiled=True)
    return column.reshape(8 * rows, PART)


def gather_plane(column):
    got = {step: shift(column, "y", 4, -step) for step in (2, 1, 3)}
    return [column, got[1], got[2], got[3]]


def send_plane(pieces, scale):
    return [shift((pieces[step - 1] * scale).astype(jnp.float16), "y", 4, step) for step in (2, 1, 3)]


def total_of(own, got, scale):
    return own + sum(g.astype(jnp.float32) for g in got) * (1.0 / scale)


def scatter_line(total, scale, applied=None):
    total = total * (scale if applied is None else applied)
    got = lax.all_to_all(total.astype(jnp.float16), "z", 0, 0, tiled=True)
    return jnp.sum(got.astype(jnp.float32), axis=0) * (1.0 / scale)


def on_device(inputs, cotangent, weight, first, second, roster_step, anchor, drift, momentum):
    q = lax.axis_index("c").astype(jnp.int32).reshape(1)
    y = lax.axis_index("y").astype(jnp.int32).reshape(1)
    x = lax.axis_index("x").astype(jnp.int32).reshape(1)
    place = jnp.concatenate([x, q])
    level = (x == q)[0]
    first_core = (q == 0)[0]
    master = weight[0]
    cast = master.astype(jnp.bfloat16)
    start = gather_line(cast[:, PART:])
    side, cross = spread(cast[:, :PART])
    drift_other = swap(drift[0], "r")
    other = swap(inputs, "c")
    block = join(place, cast[:, :PART], side, cross, start, drift_other, other)
    near = start.reshape(8, 64, PART)
    near = (near,) + spread(near)
    column = gather_plane(start)
    rest, line = next_round(column[1:], gather_line(block), near[1], near[2])
    half0 = gather_plane(line)
    rest = rest.reshape(3, 8, 64, PART)
    half1 = weave(place, near, (rest,) + spread(rest))

    delta = -(drift[0] + drift_other) / 2
    new_momentum = 0.9 * momentum + delta
    new_anchor = anchor - 0.7 * (delta + 0.9 * new_momentum)

    at = jnp.concatenate([4 * q, y])
    begun_other = project(at, other, half0[:1], (0,), None, q)
    begun = project(at, inputs, half0[:1], (0,), None, begun_other)
    pre1_other = project(at, other, half1, (0, 1, 2, 3), None, begun)
    got1 = swap(pre1_other, "c")
    pre1 = project(at, inputs, half1, (0, 1, 2, 3), None, pre1_other)
    pre0_other = project(at, other, half0[1:], (1, 2, 3), begun_other, pre1)
    got0 = swap(pre0_other, "c")
    pre0 = project(at, inputs, half0[1:], (1, 2, 3), begun, pre0_other)
    error1 = error_of(pre1, got1, cotangent, 1)
    error0 = error_of(pre0, got0, cotangent, 0)
    error1_other = swap(error1, "c")
    error0_other = swap(error0, "c")
    whole0, whole1 = gradient(at, inputs, other, (error0, error0_other, error1, error1_other))
    got0 = lax.all_to_all((whole0 * PART_SCALE).astype(jnp.float16), "y", 0, 0, tiled=True)
    low, high = whole1[:, :, :64], whole1[:, :, 64:]
    same, else_ = jnp.where(first_core, low, high), jnp.where(first_core, high, low)
    side_out = (jnp.where(level, else_, same) * PART_SCALE).astype(jnp.float16)
    cross_out = (else_ * PART_SCALE).astype(jnp.float16)
    side, cross = collect(side_out, cross_out)
    met1 = jnp.where(level, same, cross.astype(jnp.float32) * (1.0 / PART_SCALE)) + side.astype(jnp.float32) * (
        1.0 / PART_SCALE
    )
    sent1 = send_plane(met1[1:], PAIR_SCALE)

    total0 = jnp.sum(got0.astype(jnp.float32), axis=0) * (1.0 / PART_SCALE)
    total0 = scatter_line(total0, PLANE_SCALE)
    low, high = total0[:64], total0[64:]
    same, else_ = jnp.where(first_core, low, high), jnp.where(first_core, high, low)
    side, cross = collect(jnp.where(level, else_, same), else_)
    first0 = side + jnp.where(level, same, cross)
    total1 = scatter_line(total_of(met1[0], sent1, PAIR_SCALE), WHOLE_SCALE, gate(WHOLE_SCALE, total0))

    step_f = roster_step[0].astype(jnp.float32)
    corr = jnp.stack([1.0 - jnp.power(jnp.float32(0.9), step_f), 1.0 - jnp.power(jnp.float32(0.95), step_f)])
    new_weight, new_first, new_second, adam_step = adam(corr, (first0, total1), master, first[0], second[0])
    return (new_weight[None], new_first[None], new_second[None], adam_step[None], new_anchor, new_momentum)


def solution(mesh):
    fine = Mesh(mesh.devices.reshape(SIZES), AXES)
    every = ("r", "x", "y", "z", "c")
    fsdp = ("x", "y", "z", "c")
    return jax.shard_map(
        on_device,
        mesh=fine,
        in_specs=(
            P(every, None),
            P(every, None),
            P("r", fsdp, None),
            P("r", fsdp, None),
            P("r", fsdp, None),
            P("r"),
            P(fsdp, None),
            P("r", fsdp, None),
            P(fsdp, None),
        ),
        out_specs=(
            P("r", fsdp, None),
            P("r", fsdp, None),
            P("r", fsdp, None),
            P("r", fsdp, None),
            P(fsdp, None),
            P(fsdp, None),
        ),
        check_vma=False,
    )
```

```python
import functools

import jax
import jax.numpy as jnp
from jax import lax
from jax.experimental import pallas as pl
from jax.experimental.pallas import tpu as pltpu
from jax.sharding import Mesh, PartitionSpec as P

AXES = ("r", "x", "y", "z", "c")
SIZES = (2, 2, 4, 8, 2)
D = 8192
HALF = 4096
KV = 512
PART = 256
LINE = 1024
TOK = 640
PART_SCALE = 256.0
PAIR_SCALE = 128.0
PLANE_SCALE = 64.0
WHOLE_SCALE = 32.0
WIDE = 20 * 1024 * 1024
LIGHT = pl.CostEstimate(flops=1000, bytes_accessed=1000, transcendentals=0)


def swap(value, axis):
    return lax.ppermute(value, axis, [(0, 1), (1, 0)])


SIDE = [(1, 0), (2, 3), (0, 2), (3, 1)]
CROSS = [(1, 2), (2, 1)]


def spread(value):
    return lax.ppermute(value, ("x", "c"), SIDE), lax.ppermute(value, ("x", "c"), CROSS)


def collect(side, cross):
    return (
        lax.ppermute(side, ("x", "c"), [(d, s) for s, d in SIDE]),
        lax.ppermute(cross, ("x", "c"), [(d, s) for s, d in CROSS]),
    )


def shift(value, axis, size, step):
    return lax.ppermute(value, axis, [(i, (i + step) % size) for i in range(size)])


def round_kernel(a_ref, b_ref, c_ref, line_ref, side_ref, cross_ref, rows_ref, next_ref):
    for i, ref in enumerate((a_ref, b_ref, c_ref)):
        rows_ref[i] = ref[...]


def next_round(pieces, line, side, cross):
    vmem = pl.BlockSpec(memory_space=pltpu.VMEM)
    anywhere = pl.BlockSpec(memory_space=pl.ANY)
    return pl.pallas_call(
        round_kernel,
        in_specs=[vmem] * 3 + [anywhere] * 3,
        out_specs=[vmem, anywhere],
        out_shape=[
            jax.ShapeDtypeStruct((3,) + pieces[0].shape, pieces[0].dtype),
            jax.ShapeDtypeStruct(line.shape, line.dtype),
        ],
        input_output_aliases={3: 1},
        cost_estimate=LIGHT,
    )(*pieces, line, side, cross)


def put_in_order(place_ref, own_ref, side_ref, cross_ref, put):
    x, q = place_ref[0], place_ref[1]

    @pl.when(jnp.logical_and(x == 0, q == 0))
    def _():
        put(own_ref, side_ref)

    @pl.when(jnp.logical_and(x == 1, q == 1))
    def _():
        put(side_ref, own_ref)

    @pl.when(jnp.logical_and(x == 1, q == 0))
    def _():
        put(side_ref, cross_ref)

    @pl.when(jnp.logical_and(x == 0, q == 1))
    def _():
        put(cross_ref, side_ref)


def weave_kernel(place_ref, own0_ref, side0_ref, cross0_ref, own_ref, side_ref, cross_ref, o_ref):
    def put_near(low, high):
        o_ref[0, :, :64] = low[...]
        o_ref[0, :, 64:] = high[...]

    def put(low, high):
        o_ref[1:, :, :64] = low[...]
        o_ref[1:, :, 64:] = high[...]

    put_in_order(place_ref, own0_ref, side0_ref, cross0_ref, put_near)
    put_in_order(place_ref, own_ref, side_ref, cross_ref, put)


def weave(place, near, rest):
    vmem = pl.BlockSpec(memory_space=pltpu.VMEM)
    return pl.pallas_call(
        weave_kernel,
        in_specs=[pl.BlockSpec(memory_space=pltpu.SMEM)] + [vmem] * 6,
        out_specs=vmem,
        out_shape=jax.ShapeDtypeStruct((4, 8, 128, PART), jnp.bfloat16),
        compiler_params=pltpu.CompilerParams(vmem_limit_bytes=16 * 1024 * 1024),
        cost_estimate=LIGHT,
    )(place, *near, *rest)


def join_kernel(place_ref, own_ref, side_ref, cross_ref, start_ref, drift_ref, other_ref, o_ref):
    def put(low, high):
        o_ref[:64] = low[...]
        o_ref[64:] = high[...]

    put_in_order(place_ref, own_ref, side_ref, cross_ref, put)


def join(place, own, side, cross, *after):
    vmem = pl.BlockSpec(memory_space=pltpu.VMEM)
    return pl.pallas_call(
        join_kernel,
        in_specs=[pl.BlockSpec(memory_space=pltpu.SMEM)] + [vmem] * 3 + [pl.BlockSpec(memory_space=pl.ANY)] * 3,
        out_specs=vmem,
        out_shape=jax.ShapeDtypeStruct((128, PART), jnp.bfloat16),
        cost_estimate=LIGHT,
    )(place, own, side, cross, *after)


def pre_kernel(count, place_ref, *refs):
    columns, weights, o_ref = refs[:count], refs[count : 2 * count], refs[-1]
    total = None if len(refs) == 2 * count + 2 else refs[2 * count][...]
    for column, part in zip(columns, weights):
        term = jnp.dot(column[...], part[...].reshape(LINE, PART), preferred_element_type=jnp.float32)
        total = term if total is None else total + term
    o_ref[...] = total


def project(place, columns, weights, steps, begun, after):
    rows = 320

    def column_spec(step):
        return pl.BlockSpec((rows, LINE), lambda i, p: (i, p[0] + lax.rem(p[1] + step, 4)))

    out = pl.BlockSpec((rows, PART), lambda i, p: (i, 0))
    if isinstance(weights, list):
        weight_specs = [pl.BlockSpec((LINE, PART), lambda i, p: (0, 0))] * len(steps)
    else:
        weight_specs = [pl.BlockSpec((1, 8, 128, PART), lambda i, p, s=step: (s, 0, 0, 0)) for step in steps]
        weights = [weights] * len(steps)
    more = [] if begun is None else [begun]
    return pl.pallas_call(
        functools.partial(pre_kernel, len(steps)),
        grid_spec=pltpu.PrefetchScalarGridSpec(
            num_scalar_prefetch=1,
            grid=(TOK // rows,),
            in_specs=[column_spec(step) for step in steps]
            + weight_specs
            + [out] * len(more)
            + [pl.BlockSpec(memory_space=pl.ANY)],
            out_specs=out,
        ),
        out_shape=jax.ShapeDtypeStruct((TOK, PART), jnp.float32),
        compiler_params=pltpu.CompilerParams(vmem_limit_bytes=WIDE),
        cost_estimate=LIGHT,
    )(place, *[columns] * len(steps), *weights, *more, after)


def error_kernel(own_ref, got_ref, cot_ref, o_ref):
    pre = own_ref[...] + got_ref[...]
    sig = jax.nn.sigmoid(pre)
    slope = sig * (1.0 + pre * (1.0 - sig))
    o_ref[...] = (cot_ref[...].astype(jnp.float32) * slope).astype(jnp.bfloat16)


def error_of(own, got, cotangent, part):
    whole = pl.BlockSpec((TOK, PART), lambda i: (0, 0))
    return pl.pallas_call(
        error_kernel,
        grid=(1,),
        in_specs=[whole, whole, pl.BlockSpec((TOK, PART), lambda i: (0, part))],
        out_specs=whole,
        out_shape=jax.ShapeDtypeStruct((TOK, PART), jnp.bfloat16),
        compiler_params=pltpu.CompilerParams(vmem_limit_bytes=16 * 1024 * 1024),
        cost_estimate=LIGHT,
    )(own, got, cotangent)


def grad_kernel(place_ref, xo_ref, xr_ref, eo_ref, er_ref, after_ref, o_ref):
    dims = (((0,), (0,)), ((), ()))
    part = lax.dot_general(xo_ref[...], eo_ref[...], dims, preferred_element_type=jnp.float32)
    o_ref[...] = part + lax.dot_general(xr_ref[...], er_ref[...], dims, preferred_element_type=jnp.float32)


def gradient(place, own, other, err_own, err_other, after):
    x_spec = pl.BlockSpec((TOK, LINE), lambda i, p: (0, p[0] + lax.rem(p[1] + i, 4)))
    e_spec = pl.BlockSpec((TOK, PART), lambda i, p: (0, 0))
    out = pl.pallas_call(
        grad_kernel,
        grid_spec=pltpu.PrefetchScalarGridSpec(
            num_scalar_prefetch=1,
            grid=(4,),
            in_specs=[x_spec, x_spec, e_spec, e_spec, pl.BlockSpec(memory_space=pl.ANY)],
            out_specs=pl.BlockSpec((LINE, PART), lambda i, p: (i, 0)),
        ),
        out_shape=jax.ShapeDtypeStruct((HALF, PART), jnp.float32),
        compiler_params=pltpu.CompilerParams(vmem_limit_bytes=WIDE),
        cost_estimate=LIGHT,
    )(place, own, other, err_own, err_other, after)
    return out.reshape(4, 8, 128, PART)


def adam_kernel(s_ref, g0_ref, g1_ref, w_ref, m_ref, v_ref, nw_ref, nm_ref, nv_ref, st_ref):
    grad = jnp.concatenate([g0_ref[...], g1_ref[...]], axis=1)
    master = w_ref[...]
    new_first = 0.9 * m_ref[...] + 0.1 * grad
    new_second = 0.95 * v_ref[...] + 0.05 * grad * grad
    step = new_first / s_ref[0] / (jnp.sqrt(new_second / s_ref[1]) + 1e-08)
    nw_ref[...] = master - 0.0003 * (step + 0.1 * master)
    nm_ref[...] = new_first
    nv_ref[...] = new_second
    st_ref[...] = step


def adam(corr, pieces, master, first, second):
    shape = jax.ShapeDtypeStruct(master.shape, jnp.float32)
    vmem = pl.BlockSpec(memory_space=pltpu.VMEM)
    return pl.pallas_call(
        adam_kernel,
        in_specs=[pl.BlockSpec(memory_space=pltpu.SMEM)] + [vmem] * 5,
        out_specs=[vmem] * 4,
        out_shape=[shape] * 4,
    )(corr, *pieces, master, first, second)


def gather_line(block):
    rows = block.shape[0]
    column = lax.all_to_all(jnp.broadcast_to(block[None], (8, rows, PART)), "z", 0, 0, tiled=True)
    return column.reshape(8 * rows, PART)


def gather_plane(column):
    got = {step: shift(column, "y", 4, -step) for step in (2, 1, 3)}
    return [column, got[1], got[2], got[3]]


def send_plane(pieces, scale):
    return [shift((pieces[step - 1] * scale).astype(jnp.float16), "y", 4, step) for step in (2, 1, 3)]


def total_of(own, got, scale):
    return own + sum(g.astype(jnp.float32) for g in got) * (1.0 / scale)


def scatter_line(total, scale):
    got = lax.all_to_all((total * scale).astype(jnp.float16), "z", 0, 0, tiled=True)
    return jnp.sum(got.astype(jnp.float32), axis=0) * (1.0 / scale)


def scatter_by_steps(total, scale):
    z = lax.axis_index("z")
    turned = lax.dynamic_slice_in_dim(jnp.concatenate([total, total], axis=0), z, 8, 0)
    sent = (turned * scale).astype(jnp.float16)
    got = [shift(sent[step], "z", 8, step) for step in (4, 3, 5, 2, 6, 1, 7)]
    return turned[0] + sum(g.astype(jnp.float32) for g in got) * (1.0 / scale)


def on_device(inputs, cotangent, weight, first, second, roster_step, anchor, drift, momentum):
    q = lax.axis_index("c").astype(jnp.int32).reshape(1)
    y = lax.axis_index("y").astype(jnp.int32).reshape(1)
    x = lax.axis_index("x").astype(jnp.int32).reshape(1)
    place = jnp.concatenate([x, q])
    level = (x == q)[0]
    first_core = (q == 0)[0]
    master = weight[0]
    cast = master.astype(jnp.bfloat16)
    start = gather_line(cast[:, PART:])
    side, cross = spread(cast[:, :PART])
    drift_other = swap(drift[0], "r")
    other = swap(inputs, "c")
    block = join(place, cast[:, :PART], side, cross, start, drift_other, other)
    near = start.reshape(8, 64, PART)
    near = (near,) + spread(near)
    column = gather_plane(start)
    rest, line = next_round(column[1:], gather_line(block), near[1], near[2])
    half0 = gather_plane(line)
    rest = rest.reshape(3, 8, 64, PART)
    half1 = weave(place, near, (rest,) + spread(rest))

    delta = -(drift[0] + drift_other) / 2
    new_momentum = 0.9 * momentum + delta
    new_anchor = anchor - 0.7 * (delta + 0.9 * new_momentum)

    at = jnp.concatenate([4 * q, y])
    begun_other = project(at, other, half0[:1], (0,), None, q)
    begun = project(at, inputs, half0[:1], (0,), None, begun_other)
    pre1_other = project(at, other, half1, (0, 1, 2, 3), None, begun)
    got1 = swap(pre1_other, "c")
    pre1 = project(at, inputs, half1, (0, 1, 2, 3), None, pre1_other)
    pre0_other = project(at, other, half0[1:], (1, 2, 3), begun_other, pre1)
    got0 = swap(pre0_other, "c")
    pre0 = project(at, inputs, half0[1:], (1, 2, 3), begun, pre0_other)
    error1 = error_of(pre1, got1, cotangent, 1)
    error0 = error_of(pre0, got0, cotangent, 0)
    error1_other = swap(error1, "c")
    error0_other = swap(error0, "c")
    at_first = jnp.concatenate([4 * q, 0 * y])
    whole1 = gradient(at, inputs, other, error1, error1_other, pre0)
    whole0 = gradient(at_first, inputs, other, error0, error0_other, whole1)
    got0 = lax.all_to_all((whole0 * PART_SCALE).astype(jnp.float16), "y", 0, 0, tiled=True)
    low, high = whole1[:, :, :64], whole1[:, :, 64:]
    same, else_ = jnp.where(first_core, low, high), jnp.where(first_core, high, low)
    side_out = (jnp.where(level, else_, same) * PART_SCALE).astype(jnp.float16)
    cross_out = (else_ * PART_SCALE).astype(jnp.float16)
    side, cross = collect(side_out, cross_out)
    met1 = jnp.where(level, same, cross.astype(jnp.float32) * (1.0 / PART_SCALE)) + side.astype(jnp.float32) * (
        1.0 / PART_SCALE
    )
    sent1 = send_plane(met1[1:], PAIR_SCALE)

    total0 = jnp.sum(got0.astype(jnp.float32), axis=0) * (1.0 / PART_SCALE)
    total0 = scatter_line(total0, PLANE_SCALE)
    low, high = total0[:64], total0[64:]
    same, else_ = jnp.where(first_core, low, high), jnp.where(first_core, high, low)
    side, cross = collect(jnp.where(level, else_, same), else_)
    first0 = side + jnp.where(level, same, cross)
    total1 = scatter_by_steps(total_of(met1[0], sent1, PAIR_SCALE), WHOLE_SCALE)

    step_f = roster_step[0].astype(jnp.float32)
    corr = jnp.stack([1.0 - jnp.power(jnp.float32(0.9), step_f), 1.0 - jnp.power(jnp.float32(0.95), step_f)])
    new_weight, new_first, new_second, adam_step = adam(corr, (first0, total1), master, first[0], second[0])
    return (new_weight[None], new_first[None], new_second[None], adam_step[None], new_anchor, new_momentum)


def solution(mesh):
    fine = Mesh(mesh.devices.reshape(SIZES), AXES)
    every = ("r", "x", "y", "z", "c")
    fsdp = ("x", "y", "z", "c")
    return jax.shard_map(
        on_device,
        mesh=fine,
        in_specs=(
            P(every, None),
            P(every, None),
            P("r", fsdp, None),
            P("r", fsdp, None),
            P("r", fsdp, None),
            P("r"),
            P(fsdp, None),
            P("r", fsdp, None),
            P(fsdp, None),
        ),
        out_specs=(
            P("r", fsdp, None),
            P("r", fsdp, None),
            P("r", fsdp, None),
            P("r", fsdp, None),
            P(fsdp, None),
            P(fsdp, None),
        ),
        check_vma=False,
    )
```

```python
import functools

import jax
import jax.numpy as jnp
from jax import lax
from jax.experimental import pallas as pl
from jax.experimental.pallas import tpu as pltpu
from jax.sharding import Mesh, PartitionSpec as P

AXES = ("r", "x", "y", "z", "c")
SIZES = (2, 2, 4, 8, 2)
D = 8192
HALF = 4096
KV = 512
PART = 256
LINE = 1024
TOK = 640
PART_SCALE = 256.0
PAIR_SCALE = 128.0
PLANE_SCALE = 64.0
WHOLE_SCALE = 32.0
WIDE = 20 * 1024 * 1024
LIGHT = pl.CostEstimate(flops=1000, bytes_accessed=1000, transcendentals=0)


def swap(value, axis):
    return lax.ppermute(value, axis, [(0, 1), (1, 0)])


SIDE = [(1, 0), (2, 3), (0, 2), (3, 1)]
CROSS = [(1, 2), (2, 1)]


def spread(value):
    return lax.ppermute(value, ("x", "c"), SIDE), lax.ppermute(value, ("x", "c"), CROSS)


def collect(side, cross):
    return (
        lax.ppermute(side, ("x", "c"), [(d, s) for s, d in SIDE]),
        lax.ppermute(cross, ("x", "c"), [(d, s) for s, d in CROSS]),
    )


def shift(value, axis, size, step):
    return lax.ppermute(value, axis, [(i, (i + step) % size) for i in range(size)])


def stack_kernel(a_ref, b_ref, c_ref, line_ref, side_ref, cross_ref, rows_ref):
    for i, ref in enumerate((a_ref, b_ref, c_ref)):
        rows_ref[i] = ref[...]


def stack_after(pieces, *after):
    vmem = pl.BlockSpec(memory_space=pltpu.VMEM)
    return pl.pallas_call(
        stack_kernel,
        in_specs=[vmem] * 3 + [pl.BlockSpec(memory_space=pl.ANY)] * 3,
        out_specs=vmem,
        out_shape=jax.ShapeDtypeStruct((3,) + pieces[0].shape, pieces[0].dtype),
        cost_estimate=LIGHT,
    )(*pieces, *after)


def put_in_order(place_ref, own_ref, side_ref, cross_ref, put):
    x, q = place_ref[0], place_ref[1]

    @pl.when(jnp.logical_and(x == 0, q == 0))
    def _():
        put(own_ref, side_ref)

    @pl.when(jnp.logical_and(x == 1, q == 1))
    def _():
        put(side_ref, own_ref)

    @pl.when(jnp.logical_and(x == 1, q == 0))
    def _():
        put(side_ref, cross_ref)

    @pl.when(jnp.logical_and(x == 0, q == 1))
    def _():
        put(cross_ref, side_ref)


def weave_kernel(place_ref, own0_ref, side0_ref, cross0_ref, own_ref, side_ref, cross_ref, o_ref):
    def put_near(low, high):
        o_ref[0, :, :64] = low[...]
        o_ref[0, :, 64:] = high[...]

    def put(low, high):
        o_ref[1:, :, :64] = low[...]
        o_ref[1:, :, 64:] = high[...]

    put_in_order(place_ref, own0_ref, side0_ref, cross0_ref, put_near)
    put_in_order(place_ref, own_ref, side_ref, cross_ref, put)


def weave(place, near, rest):
    vmem = pl.BlockSpec(memory_space=pltpu.VMEM)
    return pl.pallas_call(
        weave_kernel,
        in_specs=[pl.BlockSpec(memory_space=pltpu.SMEM)] + [vmem] * 6,
        out_specs=vmem,
        out_shape=jax.ShapeDtypeStruct((4, 8, 128, PART), jnp.bfloat16),
        compiler_params=pltpu.CompilerParams(vmem_limit_bytes=16 * 1024 * 1024),
        cost_estimate=LIGHT,
    )(place, *near, *rest)


def join_kernel(place_ref, own_ref, side_ref, cross_ref, start_ref, drift_ref, other_ref, o_ref):
    def put(low, high):
        o_ref[:64] = low[...]
        o_ref[64:] = high[...]

    put_in_order(place_ref, own_ref, side_ref, cross_ref, put)


def join(place, own, side, cross, *after):
    vmem = pl.BlockSpec(memory_space=pltpu.VMEM)
    return pl.pallas_call(
        join_kernel,
        in_specs=[pl.BlockSpec(memory_space=pltpu.SMEM)] + [vmem] * 3 + [pl.BlockSpec(memory_space=pl.ANY)] * 3,
        out_specs=vmem,
        out_shape=jax.ShapeDtypeStruct((128, PART), jnp.bfloat16),
        cost_estimate=LIGHT,
    )(place, own, side, cross, *after)


def pre_kernel(count, place_ref, *refs):
    columns, weights, o_ref = refs[:count], refs[count : 2 * count], refs[-1]
    total = None if len(refs) == 2 * count + 2 else refs[2 * count][...]
    for column, part in zip(columns, weights):
        term = jnp.dot(column[...], part[...].reshape(LINE, PART), preferred_element_type=jnp.float32)
        total = term if total is None else total + term
    o_ref[...] = total


def project(place, columns, weights, steps, begun, after):
    rows = 320

    def column_spec(step):
        return pl.BlockSpec((rows, LINE), lambda i, p: (i, p[0] + lax.rem(p[1] + step, 4)))

    out = pl.BlockSpec((rows, PART), lambda i, p: (i, 0))
    if isinstance(weights, list):
        weight_specs = [pl.BlockSpec((LINE, PART), lambda i, p: (0, 0))] * len(steps)
    else:
        weight_specs = [pl.BlockSpec((1, 8, 128, PART), lambda i, p, s=step: (s, 0, 0, 0)) for step in steps]
        weights = [weights] * len(steps)
    more = [] if begun is None else [begun]
    return pl.pallas_call(
        functools.partial(pre_kernel, len(steps)),
        grid_spec=pltpu.PrefetchScalarGridSpec(
            num_scalar_prefetch=1,
            grid=(TOK // rows,),
            in_specs=[column_spec(step) for step in steps]
            + weight_specs
            + [out] * len(more)
            + [pl.BlockSpec(memory_space=pl.ANY)],
            out_specs=out,
        ),
        out_shape=jax.ShapeDtypeStruct((TOK, PART), jnp.float32),
        compiler_params=pltpu.CompilerParams(vmem_limit_bytes=WIDE),
        cost_estimate=LIGHT,
    )(place, *[columns] * len(steps), *weights, *more, after)


def error_kernel(own_ref, got_ref, cot_ref, o_ref):
    pre = own_ref[...] + got_ref[...]
    sig = jax.nn.sigmoid(pre)
    slope = sig * (1.0 + pre * (1.0 - sig))
    o_ref[...] = (cot_ref[...].astype(jnp.float32) * slope).astype(jnp.bfloat16)


def error_of(own, got, cotangent, part):
    whole = pl.BlockSpec((TOK, PART), lambda i: (0, 0))
    return pl.pallas_call(
        error_kernel,
        grid=(1,),
        in_specs=[whole, whole, pl.BlockSpec((TOK, PART), lambda i: (0, part))],
        out_specs=whole,
        out_shape=jax.ShapeDtypeStruct((TOK, PART), jnp.bfloat16),
        compiler_params=pltpu.CompilerParams(vmem_limit_bytes=16 * 1024 * 1024),
        cost_estimate=LIGHT,
    )(own, got, cotangent)


def grad_kernel(place_ref, xo_ref, xr_ref, eo_ref, er_ref, after_ref, o_ref):
    dims = (((0,), (0,)), ((), ()))
    part = lax.dot_general(xo_ref[...], eo_ref[...], dims, preferred_element_type=jnp.float32)
    o_ref[...] = part + lax.dot_general(xr_ref[...], er_ref[...], dims, preferred_element_type=jnp.float32)


def gradient(place, own, other, err_own, err_other, after):
    x_spec = pl.BlockSpec((TOK, LINE), lambda i, p: (0, p[0] + lax.rem(p[1] + i, 4)))
    e_spec = pl.BlockSpec((TOK, PART), lambda i, p: (0, 0))
    out = pl.pallas_call(
        grad_kernel,
        grid_spec=pltpu.PrefetchScalarGridSpec(
            num_scalar_prefetch=1,
            grid=(4,),
            in_specs=[x_spec, x_spec, e_spec, e_spec, pl.BlockSpec(memory_space=pl.ANY)],
            out_specs=pl.BlockSpec((LINE, PART), lambda i, p: (i, 0)),
        ),
        out_shape=jax.ShapeDtypeStruct((HALF, PART), jnp.float32),
        compiler_params=pltpu.CompilerParams(vmem_limit_bytes=WIDE),
        cost_estimate=LIGHT,
    )(place, own, other, err_own, err_other, after)
    return out.reshape(4, 8, 128, PART)


def adam_kernel(s_ref, g0_ref, g1_ref, w_ref, m_ref, v_ref, nw_ref, nm_ref, nv_ref, st_ref):
    grad = jnp.concatenate([g0_ref[...], g1_ref[...]], axis=1)
    master = w_ref[...]
    new_first = 0.9 * m_ref[...] + 0.1 * grad
    new_second = 0.95 * v_ref[...] + 0.05 * grad * grad
    step = new_first / s_ref[0] / (jnp.sqrt(new_second / s_ref[1]) + 1e-08)
    nw_ref[...] = master - 0.0003 * (step + 0.1 * master)
    nm_ref[...] = new_first
    nv_ref[...] = new_second
    st_ref[...] = step


def adam(corr, pieces, master, first, second):
    shape = jax.ShapeDtypeStruct(master.shape, jnp.float32)
    vmem = pl.BlockSpec(memory_space=pltpu.VMEM)
    return pl.pallas_call(
        adam_kernel,
        in_specs=[pl.BlockSpec(memory_space=pltpu.SMEM)] + [vmem] * 5,
        out_specs=[vmem] * 4,
        out_shape=[shape] * 4,
    )(corr, *pieces, master, first, second)


def gather_line(block):
    rows = block.shape[0]
    column = lax.all_to_all(jnp.broadcast_to(block[None], (8, rows, PART)), "z", 0, 0, tiled=True)
    return column.reshape(8 * rows, PART)


def gather_plane(column):
    got = {step: shift(column, "y", 4, -step) for step in (2, 1, 3)}
    return [column, got[1], got[2], got[3]]


def send_plane(pieces, scale):
    return [shift((pieces[step - 1] * scale).astype(jnp.float16), "y", 4, step) for step in (2, 1, 3)]


def total_of(own, got, scale):
    return own + sum(g.astype(jnp.float32) for g in got) * (1.0 / scale)


def scatter_line(total, scale):
    got = lax.all_to_all((total * scale).astype(jnp.float16), "z", 0, 0, tiled=True)
    return jnp.sum(got.astype(jnp.float32), axis=0) * (1.0 / scale)


def scatter_by_steps(total, scale):
    z = lax.axis_index("z")
    turned = lax.dynamic_slice_in_dim(jnp.concatenate([total, total], axis=0), z, 8, 0)
    sent = (turned * scale).astype(jnp.float16)
    got = [shift(sent[step], "z", 8, step) for step in (4, 3, 5, 2, 6, 1, 7)]
    return turned[0] + sum(g.astype(jnp.float32) for g in got) * (1.0 / scale)


def on_device(inputs, cotangent, weight, first, second, roster_step, anchor, drift, momentum):
    q = lax.axis_index("c").astype(jnp.int32).reshape(1)
    y = lax.axis_index("y").astype(jnp.int32).reshape(1)
    x = lax.axis_index("x").astype(jnp.int32).reshape(1)
    place = jnp.concatenate([x, q])
    level = (x == q)[0]
    first_core = (q == 0)[0]
    master = weight[0]
    cast = master.astype(jnp.bfloat16)
    start = gather_line(cast[:, PART:])
    side, cross = spread(cast[:, :PART])
    drift_other = swap(drift[0], "r")
    other = swap(inputs, "c")
    block = join(place, cast[:, :PART], side, cross, start, drift_other, other)
    near = start.reshape(8, 64, PART)
    near = (near,) + spread(near)
    column = gather_plane(start)
    line = gather_line(block)
    half0 = gather_plane(line)
    rest = stack_after(column[1:], line, near[1], near[2]).reshape(3, 8, 64, PART)
    half1 = weave(place, near, (rest,) + spread(rest))

    delta = -(drift[0] + drift_other) / 2
    new_momentum = 0.9 * momentum + delta
    new_anchor = anchor - 0.7 * (delta + 0.9 * new_momentum)

    at = jnp.concatenate([4 * q, y])
    begun_other = project(at, other, half0[:1], (0,), None, q)
    begun = project(at, inputs, half0[:1], (0,), None, begun_other)
    pre1_other = project(at, other, half1, (0, 1, 2, 3), None, begun)
    got1 = swap(pre1_other, "c")
    pre1 = project(at, inputs, half1, (0, 1, 2, 3), None, pre1_other)
    pre0_other = project(at, other, half0[1:], (1, 2, 3), begun_other, pre1)
    got0 = swap(pre0_other, "c")
    pre0 = project(at, inputs, half0[1:], (1, 2, 3), begun, pre0_other)
    error1 = error_of(pre1, got1, cotangent, 1)
    error0 = error_of(pre0, got0, cotangent, 0)
    error1_other = swap(error1, "c")
    error0_other = swap(error0, "c")
    at_first = jnp.concatenate([4 * q, 0 * y])
    whole1 = gradient(at, inputs, other, error1, error1_other, pre0)
    whole0 = gradient(at_first, inputs, other, error0, error0_other, whole1)
    got0 = lax.all_to_all((whole0 * PART_SCALE).astype(jnp.float16), "y", 0, 0, tiled=True)
    low, high = whole1[:, :, :64], whole1[:, :, 64:]
    same, else_ = jnp.where(first_core, low, high), jnp.where(first_core, high, low)
    side_out = (jnp.where(level, else_, same) * PART_SCALE).astype(jnp.float16)
    cross_out = (else_ * PART_SCALE).astype(jnp.float16)
    side, cross = collect(side_out, cross_out)
    met1 = jnp.where(level, same, cross.astype(jnp.float32) * (1.0 / PART_SCALE)) + side.astype(jnp.float32) * (
        1.0 / PART_SCALE
    )
    sent1 = send_plane(met1[1:], PAIR_SCALE)

    total0 = jnp.sum(got0.astype(jnp.float32), axis=0) * (1.0 / PART_SCALE)
    total0 = scatter_line(total0, PLANE_SCALE)
    low, high = total0[:64], total0[64:]
    same, else_ = jnp.where(first_core, low, high), jnp.where(first_core, high, low)
    side, cross = collect(jnp.where(level, else_, same), else_)
    first0 = side + jnp.where(level, same, cross)
    total1 = scatter_by_steps(total_of(met1[0], sent1, PAIR_SCALE), WHOLE_SCALE)

    step_f = roster_step[0].astype(jnp.float32)
    corr = jnp.stack([1.0 - jnp.power(jnp.float32(0.9), step_f), 1.0 - jnp.power(jnp.float32(0.95), step_f)])
    new_weight, new_first, new_second, adam_step = adam(corr, (first0, total1), master, first[0], second[0])
    return (new_weight[None], new_first[None], new_second[None], adam_step[None], new_anchor, new_momentum)


def solution(mesh):
    fine = Mesh(mesh.devices.reshape(SIZES), AXES)
    every = ("r", "x", "y", "z", "c")
    fsdp = ("x", "y", "z", "c")
    return jax.shard_map(
        on_device,
        mesh=fine,
        in_specs=(
            P(every, None),
            P(every, None),
            P("r", fsdp, None),
            P("r", fsdp, None),
            P("r", fsdp, None),
            P("r"),
            P(fsdp, None),
            P("r", fsdp, None),
            P(fsdp, None),
        ),
        out_specs=(
            P("r", fsdp, None),
            P("r", fsdp, None),
            P("r", fsdp, None),
            P("r", fsdp, None),
            P(fsdp, None),
            P(fsdp, None),
        ),
        check_vma=False,
    )
```
